32 devices in a mesh: snap: 1, dom: 16 (over z, y, x), rep: 2 (over core).
Axes of the slice: x: 2, y: 2, z: 4, core: 2. Of those that a mesh axis runs over, the one named last changes fastest.
Arguments:
- features: bfloat16 [1, 4096, 512], P('snap', 'dom'), may hold values from -6 to 6
- tiles: bfloat16 [1, 32, 6, 128, 128], P('snap', ('dom', 'rep')), may hold values from 0.099609375 to 1
- tile_cols: int32 [1, 32, 6], P('snap', ('dom', 'rep')), may hold values from 0 to 5, as said below
- tile_count: int32 [1, 32], P('snap', ('dom', 'rep')), may hold values from 1 to 6, as said below
- boundary_rows: int32 [1, 16, 16, 32], P('snap', 'dom'), may hold values from 0 to 255
- boundary_count: int32 [1, 16, 16], P('snap', 'dom'), may hold values from 16 to 32, as said below
- cotangent: bfloat16 [1, 4096, 512], P('snap', ('dom', 'rep')), may hold values from -6 to 6
- w_init: float32 [512, 512], P(None, 'dom'), may hold values from -0.25 to 0.25
- update_map: bfloat16 [512, 512], replicated, may hold values from -0.25 to 0.25
- reset_map: bfloat16 [512, 512], replicated, may hold values from -0.25 to 0.25
- cand_input: bfloat16 [512, 512], replicated, may hold values from -0.25 to 0.25
- cand_hidden: bfloat16 [512, 512], replicated, may hold values from -0.25 to 0.25
- update_bias: float32 [512, 512], P(None, 'dom'), may hold values from -6 to 6
- reset_bias: float32 [512, 512], P(None, 'dom'), may hold values from -6 to 6
- cand_bias: float32 [512, 512], P(None, 'dom'), may hold values from -6 to 6
Outputs:
- grad_features: bfloat16 [1, 4096, 512], P('snap', ('dom', 'rep'))
- grad_weights: float32 [1, 512, 512], P('snap', ('dom', 'rep'))
The draws below stay inside these ranges and needn't reach their ends.
Inputs may be any that keep to these rules, and one draw needn't show every extreme that they name: `tile_cols`: the 6 column blocks of one row block are distinct. `tile_count`: every row block of a partition whose index is a multiple of 4 has 6 live slots. `boundary_count`: a source and destination pair whose indices sum to a multiple of 3 has all 32 slots live.
All inputs are finite; a program needn't handle non-finite values.
Results may differ from the reference program's by a relative error of at most 0.009.
Values may be sent and summed in bfloat16 or wider, within the bound.
A program may use at most 64 MiB of HBM per device.

```python
import jax
import jax.numpy as jnp
from jax import lax

F = 512
NODE_DEV = 256
BND = 32
TILE = 128
KMAX = 6
SNAPS = 1
NODES = 4096
NCB = 6
N_DOM = 16


def draw_tile_cols(key, part):
    columns_all = NODE_DEV // TILE + NODES // NODE_DEV * BND // TILE
    draw_shape = (SNAPS, NODES // TILE, columns_all)
    scores = jax.random.randint(key, draw_shape, 0, 1 << 20, dtype=jnp.int32) * columns_all
    scores = scores + jnp.arange(columns_all, dtype=jnp.int32)
    ordering = jnp.argsort(scores, axis=-1, stable=True)
    return ordering[..., :KMAX].astype(jnp.int32)


def draw_tile_count(key, part):
    blocks_all = NODES // TILE
    drawn = jax.random.randint(key, (SNAPS, blocks_all), 1, KMAX + 1, dtype=jnp.int32)
    partition = jnp.arange(blocks_all, dtype=jnp.int32) // (NODE_DEV // TILE)
    heavy = (partition % 4 == 0)[None, :]
    return jnp.where(heavy, jnp.int32(KMAX), drawn).astype(jnp.int32)


def draw_boundary_count(key, part):
    parts_all = NODES // NODE_DEV
    drawn = jax.random.randint(key, (SNAPS, parts_all, parts_all), BND // 2, BND + 1, dtype=jnp.int32)
    source = jnp.arange(parts_all, dtype=jnp.int32)[:, None]
    target = jnp.arange(parts_all, dtype=jnp.int32)[None, :]
    filled = ((source + target) % 3 == 0)[None, :, :]
    return jnp.where(filled, jnp.int32(BND), drawn).astype(jnp.int32)


def with_ends(array, stream_key, low, high):
    place = [jax.random.randint(jax.random.fold_in(stream_key, axis), (), 0, length) for axis, length in enumerate(array.shape)]
    longest = array.shape.index(max(array.shape))
    next_to = place[:longest] + [(place[longest] + 1) % array.shape[longest]] + place[longest + 1:]
    return array.at[tuple(place)].set(low).at[tuple(next_to)].set(high)


def level_of(stream_key, extent, cuts, low, top_value):
    gain = 1.0
    for position, shards_of in cuts:
        draws = jax.random.uniform(jax.random.fold_in(jax.random.fold_in(stream_key, 6), position), (shards_of,), jnp.float32, low / len(cuts), top_value / len(cuts))
        gain = gain * jnp.repeat(jnp.exp(draws), extent[position] // shards_of).reshape((-1,) + (1,) * (len(extent) - 1 - position))
    return gain


def noise(key, dims, deviation, most, split=(), kind=jnp.bfloat16):
    result = deviation * jax.random.normal(key, dims, jnp.float32)
    if split:
        result = result * level_of(key, dims, split, -0.22, 0.18)
    return jnp.clip(result, -most, most).astype(kind)


def setup_inputs(seed: int = 0) -> dict:
    streams_of = jax.random.split(jax.random.key(seed), 16)
    features = noise(streams_of[0], (SNAPS, NODES, F), 1.0, 6.0, ((1, 16),))
    tiles = jnp.clip(0.099609375 + 0.9003906 * jax.random.uniform(streams_of[1], (SNAPS, NODES // TILE, KMAX, TILE, TILE), jnp.float32) ** level_of(streams_of[1], (SNAPS, NODES // TILE, KMAX, TILE, TILE), ((1, 32),), -0.2, 0.2), 0.099609375, 1.0).astype(jnp.bfloat16)
    tile_cols = draw_tile_cols(jax.random.fold_in(streams_of[15], 71), 0)
    tile_count = draw_tile_count(jax.random.fold_in(streams_of[15], 71), 0)
    boundary_rows = with_ends(jax.random.randint(streams_of[4], (SNAPS, N_DOM, N_DOM, BND), 0, NODE_DEV), jax.random.fold_in(streams_of[4], 1), 0, NODE_DEV - 1).astype(jnp.int32)
    boundary_count = draw_boundary_count(jax.random.fold_in(streams_of[15], 71), 0)
    cotangent = noise(streams_of[6], (SNAPS, NODES, F), 1.0, 6.0, ((1, 32),))
    w_init = noise(streams_of[7], (F, F), F ** -0.5, 0.25, ((1, 16),), jnp.float32)
    update_map = noise(streams_of[8], (F, F), F ** -0.5, 0.25)
    reset_map = noise(streams_of[9], (F, F), F ** -0.5, 0.25)
    cand_input = noise(streams_of[10], (F, F), F ** -0.5, 0.25)
    cand_hidden = noise(streams_of[11], (F, F), F ** -0.5, 0.25)
    update_bias = noise(streams_of[12], (F, F), 1.5, 6.0, ((1, 16),), jnp.float32)
    reset_bias = noise(streams_of[13], (F, F), 1.0, 6.0, ((1, 16),), jnp.float32)
    cand_bias = noise(streams_of[14], (F, F), 1.0, 6.0, ((1, 16),), jnp.float32)
    return dict(features=features, tiles=tiles, tile_cols=tile_cols, tile_count=tile_count, boundary_rows=boundary_rows, boundary_count=boundary_count, cotangent=cotangent, w_init=w_init, update_map=update_map, reset_map=reset_map, cand_input=cand_input, cand_hidden=cand_hidden, update_bias=update_bias, reset_bias=reset_bias, cand_bias=cand_bias)


def evolve_step(hidden_w, update_map, reset_map, cand_input, cand_hidden, update_bias, reset_bias, cand_bias):
    state_bf = hidden_w.astype(jnp.bfloat16)
    update = jax.nn.sigmoid(jnp.dot(update_map, state_bf, preferred_element_type=jnp.float32) + update_bias)
    reset = jax.nn.sigmoid(jnp.dot(reset_map, state_bf, preferred_element_type=jnp.float32) + reset_bias)
    gated_state = (reset * hidden_w).astype(jnp.bfloat16)
    candidate = jnp.tanh(jnp.dot(cand_input, state_bf, preferred_element_type=jnp.float32)
                         + jnp.dot(cand_hidden, gated_state, preferred_element_type=jnp.float32) + cand_bias)
    return (1.0 - update) * hidden_w + update * candidate


def pick_rows(source_rows, indices):
    return source_rows[indices]


def add_blocks(columns, grad_blocks):
    return jnp.zeros((NCB, TILE, F), jnp.float32).at[columns].add(grad_blocks)


def add_rows(grad_local, indices, returned):
    return grad_local.at[indices.reshape(-1)].add(returned.reshape(-1, F))


def reference(features, tiles, tile_cols, tile_count, boundary_rows, boundary_count, cotangent, w_init,
              update_map, reset_map, cand_input, cand_hidden, update_bias, reset_bias, cand_bias):
    def advance(hidden_w, unused):
        fresh = evolve_step(hidden_w, update_map, reset_map, cand_input, cand_hidden, update_bias, reset_bias, cand_bias)
        return fresh, fresh

    unused_last, states = lax.scan(advance, w_init, None, length=SNAPS)
    weights = states.astype(jnp.bfloat16)
    blocks_local = NODE_DEV // TILE

    def snapshot_grads(inputs):
        weight, feats, tile_vals, columns, counts, brows, bcounts, cotan = inputs
        feats = feats.reshape(N_DOM, NODE_DEV, F)
        live_slots = jnp.arange(BND, dtype=jnp.int32)[None, None, :] < bcounts[:, :, None]
        picked = jax.vmap(pick_rows)(feats, brows)
        picked = jnp.where(live_slots[..., None], picked, jnp.zeros((), jnp.bfloat16))
        halo_rows = jnp.transpose(picked, (1, 0, 2, 3)).reshape(N_DOM, N_DOM * BND, F)
        extended = jnp.concatenate([feats, halo_rows], axis=1).reshape(N_DOM, NCB, TILE, F)
        tile_vals = tile_vals.reshape(N_DOM, blocks_local, KMAX, TILE, TILE)
        columns = columns.reshape(N_DOM, blocks_local, KMAX)
        counts = counts.reshape(N_DOM, blocks_local)
        tile_live = jnp.arange(KMAX, dtype=jnp.int32)[None, None, :] < counts[..., None]
        adjacency = jnp.where(tile_live[..., None, None], tile_vals, jnp.zeros((), jnp.bfloat16))
        adj_wide = adjacency.astype(jnp.float32)
        gathered = jax.vmap(pick_rows)(extended, columns).astype(jnp.float32)
        summed = jnp.einsum('prkij,prkjf->prif', adj_wide, gathered)
        degree = jnp.sum(adj_wide, axis=(2, 4))
        aggregated = (summed / degree[..., None]).astype(jnp.bfloat16).reshape(NODES, F)
        preact = jnp.dot(aggregated, weight, preferred_element_type=jnp.float32)
        sigma_pre = jax.nn.sigmoid(preact)
        grad_pre = (cotan.astype(jnp.float32) * sigma_pre * (1.0 + preact * (1.0 - sigma_pre))).astype(jnp.bfloat16)
        grad_weight = jnp.dot(aggregated.T, grad_pre, preferred_element_type=jnp.float32)
        grad_mixed = jnp.dot(grad_pre, weight.T, preferred_element_type=jnp.float32)
        grad_summed = (grad_mixed.reshape(N_DOM, blocks_local, TILE, F) / degree[..., None]).astype(jnp.bfloat16)
        grad_blocks = jnp.einsum('prkij,prif->prkjf', adj_wide, grad_summed.astype(jnp.float32))
        grad_ext = jax.vmap(add_blocks)(columns, grad_blocks).reshape(N_DOM, NCB * TILE, F)
        grad_local = grad_ext[:, :NODE_DEV]
        grad_halo = grad_ext[:, NODE_DEV:].reshape(N_DOM, N_DOM, BND, F)
        returned = jnp.transpose(grad_halo, (1, 0, 2, 3))
        returned = jnp.where(live_slots[..., None], returned, jnp.zeros((), jnp.float32))
        grad_local = jax.vmap(add_rows)(grad_local, brows, returned)
        return grad_local.reshape(NODES, F).astype(jnp.bfloat16), grad_weight

    grad_features, grad_weights = lax.map(snapshot_grads, (weights, features, tiles, tile_cols, tile_count,
                                                           boundary_rows, boundary_count, cotangent))
    return grad_features, grad_weights
```

```python
import functools

import jax
import jax.numpy as jnp
from jax import lax
from jax.experimental import pallas as pl
from jax.experimental.pallas import tpu as pltpu
from jax.sharding import PartitionSpec as P

TILE = 128
MESH = pl.DeviceIdType.MESH
F32 = jnp.float32
BF16 = jnp.bfloat16


def dot(a, b, dims):
    return lax.dot_general(a, b, (dims, ((), ())), preferred_element_type=F32)


NN = ((1,), (0,))
NT = ((1,), (1,))
TN = ((0,), (0,))


def gru_rows(state, um, rm, ci, ch, ub, rb, cb):
    state_bf = state.astype(BF16)
    update = jax.nn.sigmoid(dot(state_bf, um, NT) + ub)
    reset = jax.nn.sigmoid(dot(state_bf, rm, NT) + rb)
    gated = (reset * state).astype(BF16)
    candidate = jnp.tanh(dot(state_bf, ci, NT) + dot(gated, ch, NT) + cb)
    return (1.0 - update) * state + update * candidate


def kernel(
    n,
    feat,
    tiles,
    inv,
    live,
    rowsel,
    cot,
    state,
    um,
    rm,
    ci,
    ch,
    ub,
    rb,
    cb,
    out_x,
    out_w,
    adj,
    ext,
    halo_out,
    cot_all,
    wt_mine,
    wt,
    agg,
    gm_out,
    gm_in,
    ret_out,
    ret_in,
    gw_out,
    gw_in,
    gws_out,
    gws_in,
    fin_out,
    fin_in,
    pair_send,
    pair_recv,
    halo_send,
    halo_recv,
    w_send,
    w_recv,
    ret_send,
    ret_recv,
    gw_send,
    gw_recv,
):
    me = lax.axis_index("dom")
    r = lax.axis_index("rep")
    other = 1 - r
    nodes, width = feat.shape
    half = width // 2
    nb = rowsel.shape[1] // n
    wrows = wt_mine.shape[0]
    per_half = half // wrows
    ncb = adj.shape[1] // TILE
    wsplit = gws_out.shape[0]

    def cols(which):
        return pl.ds(pl.multiple_of(which * half, half), half)

    def at(i, size):
        return pl.ds(pl.multiple_of(i * size, size), size)

    mine_rows = at(r, TILE)
    mine_cols, other_cols = cols(r), cols(other)

    barrier = pltpu.get_barrier_semaphore()

    def greet(i, c):
        q = lax.rem(me + i, n)
        pl.semaphore_signal(barrier, inc=1, device_id={"dom": q, "rep": other}, device_id_type=MESH)

        @pl.when(i != 0)
        def _():
            pl.semaphore_signal(barrier, inc=1, device_id={"dom": q, "rep": r}, device_id_type=MESH)

        return c

    lax.fori_loop(0, n, greet, 0)

    for c in range(ncb):
        tile = tiles[inv[c]].astype(F32) * live[c]
        adj[mine_rows, c * TILE : (c + 1) * TILE] = tile.astype(BF16)
    cot_all[mine_rows, :] = cot[:, mine_cols]

    picks = (lax.broadcasted_iota(jnp.int32, (nodes, n * nb), 0) == rowsel[...]).astype(F32).astype(BF16)
    my_feat = feat[:, mine_cols]
    halo_out[...] = dot(picks, my_feat, TN).astype(BF16)

    pl.semaphore_wait(barrier, 2 * n - 1)

    def to_pair(slot, src, dst):
        copy = pltpu.make_async_remote_copy(
            src_ref=src,
            dst_ref=dst,
            send_sem=pair_send.at[slot],
            recv_sem=pair_recv.at[slot],
            device_id={"dom": me, "rep": other},
            device_id_type=MESH,
        )
        copy.start()
        return copy

    def spread_copy(d, out_ref, in_ref, size, send_sem, recv_sem):
        q = lax.rem(me + d, n)
        return pltpu.make_async_remote_copy(
            src_ref=out_ref.at[at(q, size)],
            dst_ref=in_ref.at[at(me, size)],
            send_sem=send_sem.at[d],
            recv_sem=recv_sem.at[d],
            device_id={"dom": q, "rep": r},
            device_id_type=MESH,
        )

    def spread_start(*how):
        def go(d, c):
            spread_copy(d, *how).start()
            return c

        lax.fori_loop(1, n, go, 0)

    def spread_wait(out_ref, in_ref, size, send_sem, recv_sem):
        def go(d, c):
            src = lax.rem(me + n - d, n)
            pltpu.make_async_remote_copy(
                src_ref=out_ref.at[at(src, size)],
                dst_ref=in_ref.at[at(src, size)],
                send_sem=send_sem.at[d],
                recv_sem=recv_sem.at[d],
                device_id={"dom": src, "rep": r},
                device_id_type=MESH,
            ).wait_recv()
            return c

        lax.fori_loop(1, n, go, 0)

    def spread_drain(*how):
        def go(d, c):
            spread_copy(d, *how).wait_send()
            return c

        lax.fori_loop(1, n, go, 0)

    adj_copy = to_pair(0, adj.at[mine_rows], adj.at[mine_rows])
    cot_copy = to_pair(1, cot.at[:, other_cols], cot_all.at[mine_rows])
    halo = (halo_out, ext.at[pl.ds(nodes, n * nb)], nb, halo_send, halo_recv)
    spread_start(*halo)

    ext[pl.ds(0, nodes), :] = my_feat
    ext[pl.ds(pl.multiple_of(nodes + me * nb, nb), nb), :] = halo_out[at(me, nb), :]

    fresh = gru_rows(state[...], um[...], rm[...], ci[...], ch[...], ub[...], rb[...], cb[...])
    wt_mine[...] = fresh.astype(BF16)
    h = me // per_half
    place = lax.rem(me, per_half)

    def w_copy(i):
        d = 2 * i + r
        q = lax.rem(me + d, n)
        return d, pltpu.make_async_remote_copy(
            src_ref=wt_mine,
            dst_ref=wt.at[at(place, wrows)],
            send_sem=w_send.at[i],
            recv_sem=w_recv.at[place],
            device_id={"dom": q, "rep": h},
            device_id_type=MESH,
        )

    def w_start(i, c):
        d, copy = w_copy(i)

        @pl.when(d != 0)
        def _():
            copy.start()

        return c

    lax.fori_loop(0, n // 2, w_start, 0)

    @pl.when(h == r)
    def _():
        wt[at(place, wrows), :] = wt_mine[...]

    adj_copy.wait()
    full = adj[...]
    degree = jnp.sum(full.astype(F32), axis=1, keepdims=True)

    spread_wait(*halo)
    summed = dot(full, ext[...], NN)
    agg[:, mine_cols] = (summed / degree).astype(BF16)
    agg_copy = to_pair(2, agg.at[:, mine_cols], agg.at[:, mine_cols])

    def w_wait(i, c):
        src = r * per_half + i

        @pl.when(src != me)
        def _():
            pltpu.make_async_remote_copy(
                src_ref=wt_mine,
                dst_ref=wt.at[at(i, wrows)],
                send_sem=w_send.at[0],
                recv_sem=w_recv.at[i],
                device_id={"dom": src, "rep": other},
                device_id_type=MESH,
            ).wait_recv()

        return c

    lax.fori_loop(0, per_half, w_wait, 0)
    cot_copy.wait()
    agg_copy.wait()

    weights = wt[...]
    aggregated = agg[...]
    preact = dot(aggregated, weights, NT)
    sig = jax.nn.sigmoid(preact)
    grad_pre = (cot_all[...].astype(F32) * sig * (1.0 + preact * (1.0 - sig))).astype(BF16)
    mixed = dot(grad_pre, weights, NN)
    gm_out[...] = jnp.where(r == 0, mixed[:, half:], mixed[:, :half]).astype(BF16)
    mixed_mine = jnp.where(r == 0, mixed[:, :half], mixed[:, half:])
    gm_copy = to_pair(3, gm_out, gm_in)

    gw_out[...] = dot(aggregated, grad_pre, TN).astype(BF16)
    gw = (gw_out, gw_in, wrows, gw_send, gw_recv)

    gm_copy.wait()
    grad_summed = ((mixed_mine + gm_in[...].astype(F32)) / degree).astype(BF16)
    grad_halo = dot(full[:, nodes:], grad_summed, TN)
    ret_out[...] = grad_halo.astype(BF16)
    ret = (ret_out, ret_in, nb, ret_send, ret_recv)
    spread_start(*ret)
    spread_start(*gw)
    ret_in[at(me, nb), :] = ret_out[at(me, nb), :]
    gw_in[at(me, wrows), :] = gw_out[at(me, wrows), :]
    grad_local = dot(full[:, :nodes], grad_summed, TN)

    spread_wait(*ret)
    total = (grad_local + dot(picks, ret_in[...], NN)).astype(BF16)
    fin_out[...] = jnp.where(r == 0, total[TILE:], total[:TILE])
    fin_copy = to_pair(4, fin_out, fin_in)
    out_x[:, mine_cols] = jnp.where(r == 0, total[:TILE], total[TILE:])

    spread_wait(*gw)
    acc = gw_in[0:wrows, :].astype(F32)
    for p in range(1, n):
        acc = acc + gw_in[p * wrows : (p + 1) * wrows, :].astype(F32)
    gws_out[...] = jnp.where(r == 0, acc[wsplit:], acc[:wsplit])
    gws_copy = to_pair(5, gws_out, gws_in)
    out_w[:, mine_cols] = jnp.where(r == 0, acc[:wsplit], acc[wsplit:])

    fin_copy.wait()
    out_x[:, other_cols] = fin_in[...]
    gws_copy.wait()
    out_w[:, other_cols] = gws_in[...]

    def w_drain(i, c):
        d, copy = w_copy(i)

        @pl.when(d != 0)
        def _():
            copy.wait_send()

        return c

    lax.fori_loop(0, n // 2, w_drain, 0)
    spread_drain(*halo)
    spread_drain(*ret)
    spread_drain(*gw)


def local(
    features,
    tiles,
    tile_cols,
    tile_count,
    boundary_rows,
    boundary_count,
    cotangent,
    w_init,
    update_map,
    reset_map,
    cand_input,
    cand_hidden,
    update_bias,
    reset_bias,
    cand_bias,
):
    assert features.shape[0] == 1 and tiles.shape[1] == 1
    n = lax.axis_size("dom")
    nodes, width = features.shape[1:]
    half = width // 2
    nb = boundary_rows.shape[-1]
    kmax = tiles.shape[2]
    ncb = (nodes + n * nb) // TILE
    wrows = width // n
    maps = (update_map, reset_map, cand_input, cand_hidden)
    biases = (update_bias.T, reset_bias.T, cand_bias.T)
    state = w_init.T
    if lax.axis_size("snap") > 1:
        state = lax.fori_loop(
            0, lax.axis_index("snap"), lambda i, s: gru_rows(s, *maps, *biases), state
        )

    ks = jnp.arange(kmax, dtype=jnp.int32)
    hit = (tile_cols[0, 0][None, :] == jnp.arange(ncb, dtype=jnp.int32)[:, None]) & (
        ks < tile_count[0, 0]
    )[None, :]
    inv = jnp.sum(jnp.where(hit, ks[None, :], 0), axis=1)
    live = jnp.any(hit, axis=1).astype(F32)
    slots = jnp.arange(nb, dtype=jnp.int32)
    rowsel = jnp.where(slots[None, :] < boundary_count[0, 0][:, None], boundary_rows[0, 0], -1)
    rowsel = rowsel.reshape(1, n * nb)

    vmem = pl.BlockSpec(memory_space=pltpu.VMEM)
    smem = pl.BlockSpec(memory_space=pltpu.SMEM)
    dma = pltpu.SemaphoreType.DMA
    out_x, out_w = pl.pallas_call(
        functools.partial(kernel, n),
        out_shape=(
            jax.ShapeDtypeStruct((TILE, width), BF16),
            jax.ShapeDtypeStruct((wrows // 2, width), F32),
        ),
        in_specs=[vmem, vmem, smem, smem] + [vmem] * 10,
        out_specs=(vmem, vmem),
        scratch_shapes=[
            pltpu.VMEM((nodes, ncb * TILE), BF16),
            pltpu.VMEM((ncb * TILE, half), BF16),
            pltpu.VMEM((n * nb, half), BF16),
            pltpu.VMEM((nodes, half), BF16),
            pltpu.VMEM((wrows, width), BF16),
            pltpu.VMEM((half, width), BF16),
            pltpu.VMEM((nodes, width), BF16),
            pltpu.VMEM((nodes, half), BF16),
            pltpu.VMEM((nodes, half), BF16),
            pltpu.VMEM((n * nb, half), BF16),
            pltpu.VMEM((n * nb, half), BF16),
            pltpu.VMEM((width, half), BF16),
            pltpu.VMEM((width, half), BF16),
            pltpu.VMEM((wrows // 2, half), F32),
            pltpu.VMEM((wrows // 2, half), F32),
            pltpu.VMEM((TILE, half), BF16),
            pltpu.VMEM((TILE, half), BF16),
            dma((6,)),
            dma((6,)),
            dma((n,)),
            dma((n,)),
            dma((n // 2,)),
            dma((n // 2,)),
            dma((n,)),
            dma((n,)),
            dma((n,)),
            dma((n,)),
        ],
        compiler_params=pltpu.CompilerParams(
            collective_id=0, has_side_effects=True, vmem_limit_bytes=40 << 20
        ),
    )(features[0], tiles[0, 0], inv, live, rowsel, cotangent[0], state, *maps, *biases)
    return out_x[None], out_w[None]


def solution(mesh):
    in_specs = (
        P("snap", "dom", None),
        P("snap", ("dom", "rep"), None, None, None),
        P("snap", ("dom", "rep"), None),
        P("snap", ("dom", "rep")),
        P("snap", "dom", None, None),
        P("snap", "dom", None),
        P("snap", ("dom", "rep"), None),
        P(None, "dom"),
        P(),
        P(),
        P(),
        P(),
        P(None, "dom"),
        P(None, "dom"),
        P(None, "dom"),
    )
    out_specs = (P("snap", ("dom", "rep"), None), P("snap", ("dom", "rep"), None))
    return jax.shard_map(local, mesh=mesh, in_specs=in_specs, out_specs=out_specs, check_vma=False)
```

```python
import functools

import jax
import jax.numpy as jnp
from jax import lax
from jax.experimental import pallas as pl
from jax.experimental.pallas import tpu as pltpu
from jax.sharding import PartitionSpec as P

TILE = 128
MESH = pl.DeviceIdType.MESH
F32 = jnp.float32
BF16 = jnp.bfloat16


def dot(a, b, dims):
    return lax.dot_general(a, b, (dims, ((), ())), preferred_element_type=F32)


NN = ((1,), (0,))
NT = ((1,), (1,))
TN = ((0,), (0,))


def gru_rows(state, um, rm, ci, ch, ub, rb, cb):
    state_bf = state.astype(BF16)
    update = jax.nn.sigmoid(dot(state_bf, um, NT) + ub)
    reset = jax.nn.sigmoid(dot(state_bf, rm, NT) + rb)
    gated = (reset * state).astype(BF16)
    candidate = jnp.tanh(dot(state_bf, ci, NT) + dot(gated, ch, NT) + cb)
    return (1.0 - update) * state + update * candidate


def kernel(
    n,
    lo,
    cols_ref,
    count_ref,
    *refs,
):
    (
        feat_hbm, tiles_hbm, brows_hbm, bcount_hbm, cot_hbm, state_hbm,
        um_hbm, rm_hbm, ci_hbm, ch_hbm, ub_hbm, rb_hbm, cb_hbm,
        out_x, out_w,
        feat, tiles, brows, bcount, cot, state, um, rm, ci, ch, ub, rb, cb,
        in_sem,
        picks, adj, ext, halo_out, cot_all, wt_mine, wt, agg, gm_out, gm_in,
        ret_out, ret_in, gw_out, gw1_in, gw_mid, gw2_in, gws_out, gws_in, fin_out, fin_in,
        pair_send, pair_recv, halo_send, halo_recv, w1_send, w2_send, w_recv,
        ret_send, ret_recv, gw1_send, gw1_recv, gw2_send, gw2_recv,
    ) = refs
    me = lax.axis_index("dom")
    r = lax.axis_index("rep")
    other = 1 - r
    hi = n // lo
    z, l = me // lo, lax.rem(me, lo)
    nodes, width = feat.shape
    half = width // 2
    nb = brows.shape[1]
    wrows = wt_mine.shape[0]
    kmax = tiles.shape[0]
    ncb = adj.shape[1] // TILE
    wsplit = gws_out.shape[0]

    hbm = (feat_hbm, brows_hbm, bcount_hbm, tiles_hbm, cot_hbm, state_hbm,
           um_hbm, rm_hbm, ci_hbm, ch_hbm, ub_hbm, rb_hbm, cb_hbm)
    vmem = (feat, brows, bcount, tiles, cot, state, um, rm, ci, ch, ub, rb, cb)
    loads = [pltpu.make_async_copy(x, y, in_sem.at[i]) for i, (x, y) in enumerate(zip(hbm, vmem))]
    for load in loads:
        load.start()

    def cols(which):
        return pl.ds(pl.multiple_of(which * half, half), half)

    def at(i, size):
        return pl.ds(pl.multiple_of(i * size, size), size)

    def remote(src, dst, send_sem, recv_sem, dom, rep):
        return pltpu.make_async_remote_copy(
            src_ref=src,
            dst_ref=dst,
            send_sem=send_sem,
            recv_sem=recv_sem,
            device_id={"dom": dom, "rep": rep},
            device_id_type=MESH,
        )

    mine_rows = at(r, TILE)
    mine_cols, other_cols = cols(r), cols(other)

    barrier = pltpu.get_barrier_semaphore()

    def greet(i, c):
        q = lax.rem(me + i, n)
        pl.semaphore_signal(barrier, inc=1, device_id={"dom": q, "rep": other}, device_id_type=MESH)

        @pl.when(i != 0)
        def _():
            pl.semaphore_signal(barrier, inc=1, device_id={"dom": q, "rep": r}, device_id_type=MESH)

        return c

    lax.fori_loop(0, n, greet, 0)

    for load in loads[:3]:
        load.wait()
    lane = lax.broadcasted_iota(jnp.int32, (nb, n * nb), 1)
    spread_slot = (lax.rem(lane, nb) == lax.broadcasted_iota(jnp.int32, (nb, n * nb), 0)).astype(F32)
    lane_q = lax.broadcasted_iota(jnp.int32, (n, n * nb), 1)
    in_q = lax.div(lane_q, nb) == lax.broadcasted_iota(jnp.int32, (n, n * nb), 0)
    by_slot = dot(brows[...].astype(F32).astype(BF16), spread_slot.astype(BF16), NN)
    row_of = jnp.sum(jnp.where(in_q, by_slot, 0.0), axis=0, keepdims=True)
    counts = jnp.broadcast_to(bcount[...].astype(F32), (n, n)).astype(BF16)
    limit = dot(counts, in_q.astype(F32).astype(BF16), NN)[0:1]
    slot = lax.rem(lane_q[0:1], nb).astype(F32)
    rowsel = jnp.where(slot < limit, row_of, -1.0).astype(jnp.int32)
    picks[...] = (lax.broadcasted_iota(jnp.int32, (nodes, n * nb), 0) == rowsel).astype(F32).astype(BF16)
    halo_out[...] = dot(picks[...], feat[:, mine_cols], TN).astype(BF16)

    for load in loads[3:5]:
        load.wait()
    for c in range(ncb):
        index = jnp.int32(0)
        live = jnp.float32(0.0)
        for k in range(kmax):
            hit = (cols_ref[0, k] == c) & (k < count_ref[0, 0])
            index = jnp.where(hit, k, index)
            live = jnp.where(hit, 1.0, live)
        adj[mine_rows, c * TILE : (c + 1) * TILE] = (tiles[index].astype(F32) * live).astype(BF16)
    cot_all[mine_rows, :] = cot[:, mine_cols]

    pl.semaphore_wait(barrier, 2 * n - 1)

    def to_pair(slot, src, dst):
        copy = remote(src, dst, pair_send.at[slot], pair_recv.at[slot], me, other)
        copy.start()
        return copy

    def spread_copy(d, out_ref, in_ref, send_sem, recv_sem):
        q = lax.rem(me + d, n)
        return remote(
            out_ref.at[at(q, nb)], in_ref.at[at(me, nb)], send_sem.at[d], recv_sem.at[d], q, r
        )

    def spread_start(*how):
        def go(d, c):
            spread_copy(d, *how).start()
            return c

        lax.fori_loop(1, n, go, 0)

    def spread_wait(out_ref, in_ref, send_sem, recv_sem):
        def go(d, c):
            src = lax.rem(me + n - d, n)
            block = at(src, nb)
            remote(
                out_ref.at[block], in_ref.at[block], send_sem.at[d], recv_sem.at[d], src, r
            ).wait_recv()
            return c

        lax.fori_loop(1, n, go, 0)

    def spread_drain(*how):
        def go(d, c):
            spread_copy(d, *how).wait_send()
            return c

        lax.fori_loop(1, n, go, 0)

    halo = (halo_out, ext.at[pl.ds(nodes, n * nb)], halo_send, halo_recv)
    spread_start(*halo)
    adj_copy = to_pair(0, adj.at[mine_rows], adj.at[mine_rows])
    cot_copy = to_pair(1, cot.at[:, other_cols], cot_all.at[mine_rows])

    for load in loads[5:]:
        load.wait()
    fresh = gru_rows(state[...], um[...], rm[...], ci[...], ch[...], ub[...], rb[...], cb[...])
    wt_mine[...] = fresh.astype(BF16)
    zh = hi // 2
    h = z // zh
    place = lax.rem(z, zh) * lo + l

    def w1_copy(i):
        dz = 2 * i + r
        q = lax.rem(z + dz, hi) * lo + l
        return dz, remote(
            wt_mine, wt.at[at(place, wrows)], w1_send.at[i], w_recv.at[place], q, h
        )

    for i in range(zh):
        dz, copy = w1_copy(i)

        @pl.when(dz != 0)
        def _():
            copy.start()

    @pl.when(h == r)
    def _():
        wt[at(place, wrows), :] = wt_mine[...]

    ext[pl.ds(0, nodes), :] = feat[:, mine_cols]
    ext[pl.ds(pl.multiple_of(nodes + me * nb, nb), nb), :] = halo_out[at(me, nb), :]

    adj_copy.wait()
    degree = jnp.sum(adj[...].astype(F32), axis=1, keepdims=True)

    def w_arrival(block):
        here = wt.at[at(block, wrows)]
        return remote(here, here, w1_send.at[0], w_recv.at[block], me, other)

    def w2_copy(i, dl):
        block = i * lo + l
        here = wt.at[at(block, wrows)]
        q = z * lo + lax.rem(l + dl, lo)
        return remote(here, here, w2_send.at[i * lo + dl], w_recv.at[block], q, r)

    for i in range(zh):

        @pl.when(r * zh + i != z)
        def _():
            w_arrival(i * lo + l).wait_recv()

        for dl in range(1, lo):
            w2_copy(i, dl).start()

    spread_wait(*halo)
    agg[:, mine_cols] = (dot(adj[...], ext[...], NN) / degree).astype(BF16)
    agg_copy = to_pair(2, agg.at[:, mine_cols], agg.at[:, mine_cols])

    for i in range(zh):
        for dl in range(1, lo):
            w_arrival(i * lo + lax.rem(l + dl, lo)).wait_recv()
    cot_copy.wait()
    agg_copy.wait()

    preact = dot(agg[...], wt[...], NT)
    sig = jax.nn.sigmoid(preact)
    grad_pre = (cot_all[...].astype(F32) * sig * (1.0 + preact * (1.0 - sig))).astype(BF16)
    mixed = dot(grad_pre, wt[...], NN)
    gm_out[...] = jnp.where(r == 0, mixed[:, half:], mixed[:, :half]).astype(BF16)
    mixed_mine = jnp.where(r == 0, mixed[:, :half], mixed[:, half:])
    gm_copy = to_pair(3, gm_out, gm_in)

    partial = dot(agg[...], grad_pre, TN)
    for p in range(n):
        to = ((p % lo) * hi + p // lo) * wrows
        gw_out[to : to + wrows, :] = partial[p * wrows : (p + 1) * wrows].astype(BF16)
    rows1 = hi * wrows

    def gw1_copy(dl):
        to = lax.rem(l + dl, lo)
        return remote(
            gw_out.at[at(to, rows1)], gw1_in.at[dl], gw1_send.at[dl], gw1_recv.at[dl], z * lo + to, r
        )

    def gw2_copy(dz):
        to = lax.rem(z + dz, hi)
        return remote(
            gw_mid.at[at(to, wrows)], gw2_in.at[dz], gw2_send.at[dz], gw2_recv.at[dz], to * lo + l, r
        )

    gm_copy.wait()
    grad_summed = ((mixed_mine + gm_in[...].astype(F32)) / degree).astype(BF16)
    ret_out[...] = dot(adj[:, nodes:], grad_summed, TN).astype(BF16)
    ret = (ret_out, ret_in, ret_send, ret_recv)
    spread_start(*ret)
    for dl in range(1, lo):
        gw1_copy(dl).start()
    ret_in[at(me, nb), :] = ret_out[at(me, nb), :]
    grad_local = dot(adj[:, :nodes], grad_summed, TN)

    acc = gw_out[at(l, rows1), :].astype(F32)
    for dl in range(1, lo):
        gw1_copy(dl).wait_recv()
        acc = acc + gw1_in[dl].astype(F32)
    gw_mid[...] = acc.astype(BF16)
    for dz in range(1, hi):
        gw2_copy(dz).start()

    spread_wait(*ret)
    total = (grad_local + dot(picks[...], ret_in[...], NN)).astype(BF16)
    fin_out[...] = jnp.where(r == 0, total[TILE:], total[:TILE])
    fin_copy = to_pair(4, fin_out, fin_in)
    out_x[:, mine_cols] = jnp.where(r == 0, total[:TILE], total[TILE:])

    acc = gw_mid[at(z, wrows), :].astype(F32)
    for dz in range(1, hi):
        gw2_copy(dz).wait_recv()
        acc = acc + gw2_in[dz].astype(F32)
    gws_out[...] = jnp.where(r == 0, acc[wsplit:], acc[:wsplit])
    gws_copy = to_pair(5, gws_out, gws_in)
    out_w[:, mine_cols] = jnp.where(r == 0, acc[:wsplit], acc[wsplit:])

    fin_copy.wait()
    out_x[:, other_cols] = fin_in[...]
    gws_copy.wait()
    out_w[:, other_cols] = gws_in[...]

    for i in range(zh):
        dz, copy = w1_copy(i)

        @pl.when(dz != 0)
        def _():
            copy.wait_send()

        for dl in range(1, lo):
            w2_copy(i, dl).wait_send()
    for dl in range(1, lo):
        gw1_copy(dl).wait_send()
    for dz in range(1, hi):
        gw2_copy(dz).wait_send()
    spread_drain(*halo)
    spread_drain(*ret)


def local(
    features,
    tiles,
    tile_cols,
    tile_count,
    boundary_rows,
    boundary_count,
    cotangent,
    w_init,
    update_map,
    reset_map,
    cand_input,
    cand_hidden,
    update_bias,
    reset_bias,
    cand_bias,
):
    assert features.shape[0] == 1 and tiles.shape[1] == 1
    n = lax.axis_size("dom")
    nodes, width = features.shape[1:]
    half = width // 2
    nb = boundary_rows.shape[-1]
    ncb = (nodes + n * nb) // TILE
    wrows = width // n
    maps = (update_map, reset_map, cand_input, cand_hidden)
    biases = (update_bias.T, reset_bias.T, cand_bias.T)
    state = w_init.T
    if lax.axis_size("snap") > 1:
        state = lax.fori_loop(
            0, lax.axis_index("snap"), lambda i, s: gru_rows(s, *maps, *biases), state
        )

    lo = 4
    hi = n // lo
    zh = hi // 2
    arrays = (features[0], tiles[0, 0], boundary_rows[0, 0], boundary_count[0], cotangent[0], state)
    arrays = arrays + maps + biases
    hbm = pl.BlockSpec(memory_space=pltpu.HBM)
    vmem = pl.BlockSpec(memory_space=pltpu.VMEM)
    smem = pl.BlockSpec(memory_space=pltpu.SMEM)
    dma = pltpu.SemaphoreType.DMA
    out_x, out_w = pl.pallas_call(
        functools.partial(kernel, n, lo),
        out_shape=(
            jax.ShapeDtypeStruct((TILE, width), BF16),
            jax.ShapeDtypeStruct((wrows // 2, width), F32),
        ),
        in_specs=[smem, smem] + [hbm] * len(arrays),
        out_specs=(vmem, vmem),
        scratch_shapes=[pltpu.VMEM(x.shape, x.dtype) for x in arrays]
        + [
            dma((len(arrays),)),
            pltpu.VMEM((nodes, n * nb), BF16),
            pltpu.VMEM((nodes, ncb * TILE), BF16),
            pltpu.VMEM((ncb * TILE, half), BF16),
            pltpu.VMEM((n * nb, half), BF16),
            pltpu.VMEM((nodes, half), BF16),
            pltpu.VMEM((wrows, width), BF16),
            pltpu.VMEM((half, width), BF16),
            pltpu.VMEM((nodes, width), BF16),
            pltpu.VMEM((nodes, half), BF16),
            pltpu.VMEM((nodes, half), BF16),
            pltpu.VMEM((n * nb, half), BF16),
            pltpu.VMEM((n * nb, half), BF16),
            pltpu.VMEM((width, half), BF16),
            pltpu.VMEM((lo, hi * wrows, half), BF16),
            pltpu.VMEM((hi * wrows, half), BF16),
            pltpu.VMEM((hi, wrows, half), BF16),
            pltpu.VMEM((wrows // 2, half), F32),
            pltpu.VMEM((wrows // 2, half), F32),
            pltpu.VMEM((TILE, half), BF16),
            pltpu.VMEM((TILE, half), BF16),
            dma((6,)),
            dma((6,)),
            dma((n,)),
            dma((n,)),
            dma((zh,)),
            dma((zh * lo,)),
            dma((zh * lo,)),
            dma((n,)),
            dma((n,)),
            dma((lo,)),
            dma((lo,)),
            dma((hi,)),
            dma((hi,)),
        ],
        compiler_params=pltpu.CompilerParams(
            collective_id=0, has_side_effects=True, vmem_limit_bytes=40 << 20
        ),
    )(tile_cols[0], tile_count, *arrays)
    return out_x[None], out_w[None]


def solution(mesh):
    in_specs = (
        P("snap", "dom", None),
        P("snap", ("dom", "rep"), None, None, None),
        P("snap", ("dom", "rep"), None),
        P("snap", ("dom", "rep")),
        P("snap", "dom", None, None),
        P("snap", "dom", None),
        P("snap", ("dom", "rep"), None),
        P(None, "dom"),
        P(),
        P(),
        P(),
        P(),
        P(None, "dom"),
        P(None, "dom"),
        P(None, "dom"),
    )
    out_specs = (P("snap", ("dom", "rep"), None), P("snap", ("dom", "rep"), None))
    return jax.shard_map(local, mesh=mesh, in_specs=in_specs, out_specs=out_specs, check_vma=False)
```

```python
import functools

import jax
import jax.numpy as jnp
from jax import lax
from jax.experimental import pallas as pl
from jax.experimental.pallas import tpu as pltpu
from jax.sharding import PartitionSpec as P

TILE = 128
MESH = pl.DeviceIdType.MESH
F32 = jnp.float32
BF16 = jnp.bfloat16


def dot(a, b, dims):
    return lax.dot_general(a, b, (dims, ((), ())), preferred_element_type=F32)


NN = ((1,), (0,))
NT = ((1,), (1,))
TN = ((0,), (0,))


def gru_rows(state, um, rm, ci, ch, ub, rb, cb):
    state_bf = state.astype(BF16)
    update = jax.nn.sigmoid(dot(state_bf, um, NT) + ub)
    reset = jax.nn.sigmoid(dot(state_bf, rm, NT) + rb)
    gated = (reset * state).astype(BF16)
    candidate = jnp.tanh(dot(state_bf, ci, NT) + dot(gated, ch, NT) + cb)
    return (1.0 - update) * state + update * candidate


def kernel(
    n,
    lo,
    cols_ref,
    count_ref,
    *refs,
):
    (
        feat_hbm, tiles_hbm, brows_hbm, bcount_hbm, cot_hbm, state_hbm,
        um_hbm, rm_hbm, ci_hbm, ch_hbm, ub_hbm, rb_hbm, cb_hbm,
        out_x, out_w,
        feat, tiles, brows, bcount, cot, state, um, rm, ci, ch, ub, rb, cb,
        in_sem,
        picks, adj, ext, halo_out, cot_all, wt_mine, wt, agg, gm_out, gm_in,
        ret_out, ret_in, gw_out, gw1_in, gw_mid, gw2_in, gws_out, gws_in, fin_out, fin_in,
        pair_send, pair_recv, halo_send, halo_recv, w1_send, w2_send, w_recv,
        ret_send, ret_recv, gw1_send, gw1_recv, gw2_send, gw2_recv,
    ) = refs
    me = lax.axis_index("dom")
    r = lax.axis_index("rep")
    other = 1 - r
    hi = n // lo
    z, l = me // lo, lax.rem(me, lo)
    nodes, width = feat.shape
    half = width // 2
    nb = brows.shape[1]
    wrows = wt_mine.shape[0]
    kmax = tiles.shape[0]
    ncb = adj.shape[1] // TILE
    wsplit = gws_out.shape[0]

    hbm = (feat_hbm, brows_hbm, bcount_hbm, tiles_hbm, cot_hbm, state_hbm,
           um_hbm, rm_hbm, ci_hbm, ch_hbm, ub_hbm, rb_hbm, cb_hbm)
    vmem = (feat, brows, bcount, tiles, cot, state, um, rm, ci, ch, ub, rb, cb)
    loads = [pltpu.make_async_copy(x, y, in_sem.at[i]) for i, (x, y) in enumerate(zip(hbm, vmem))]
    for load in loads:
        load.start()

    def cols(which):
        return pl.ds(pl.multiple_of(which * half, half), half)

    def at(i, size):
        return pl.ds(pl.multiple_of(i * size, size), size)

    def remote(src, dst, send_sem, recv_sem, dom, rep):
        return pltpu.make_async_remote_copy(
            src_ref=src,
            dst_ref=dst,
            send_sem=send_sem,
            recv_sem=recv_sem,
            device_id={"dom": dom, "rep": rep},
            device_id_type=MESH,
        )

    mine_rows = at(r, TILE)
    mine_cols, other_cols = cols(r), cols(other)

    barrier = pltpu.get_barrier_semaphore()

    pl.semaphore_signal(barrier, inc=1, device_id={"dom": me, "rep": other}, device_id_type=MESH)

    def greet(i, c):
        q = lax.rem(me + i, n)
        pl.semaphore_signal(barrier, inc=1, device_id={"dom": q, "rep": r}, device_id_type=MESH)
        return c

    lax.fori_loop(1, n, greet, 0)

    for load in loads[:3]:
        load.wait()
    lane = lax.broadcasted_iota(jnp.int32, (nb, n * nb), 1)
    spread_slot = (lax.rem(lane, nb) == lax.broadcasted_iota(jnp.int32, (nb, n * nb), 0)).astype(F32)
    lane_q = lax.broadcasted_iota(jnp.int32, (n, n * nb), 1)
    in_q = lax.div(lane_q, nb) == lax.broadcasted_iota(jnp.int32, (n, n * nb), 0)
    by_slot = dot(brows[...].astype(F32).astype(BF16), spread_slot.astype(BF16), NN)
    row_of = jnp.sum(jnp.where(in_q, by_slot, 0.0), axis=0, keepdims=True)
    counts = jnp.broadcast_to(bcount[...].astype(F32), (n, n)).astype(BF16)
    limit = dot(counts, in_q.astype(F32).astype(BF16), NN)[0:1]
    slot = lax.rem(lane_q[0:1], nb).astype(F32)
    rowsel = jnp.where(slot < limit, row_of, -1.0).astype(jnp.int32)
    picks[...] = (lax.broadcasted_iota(jnp.int32, (nodes, n * nb), 0) == rowsel).astype(F32).astype(BF16)
    halo_out[...] = dot(picks[...], feat[:, mine_cols], TN).astype(BF16)

    for load in loads[3:5]:
        load.wait()
    for c in range(ncb):
        index = jnp.int32(0)
        live = jnp.float32(0.0)
        for k in range(kmax):
            hit = (cols_ref[0, k] == c) & (k < count_ref[0, 0])
            index = jnp.where(hit, k, index)
            live = jnp.where(hit, 1.0, live)
        adj[mine_rows, c * TILE : (c + 1) * TILE] = (tiles[index].astype(F32) * live).astype(BF16)
    cot_all[mine_rows, :] = cot[:, mine_cols]

    for load in loads[5:]:
        load.wait()
    fresh = gru_rows(state[...], um[...], rm[...], ci[...], ch[...], ub[...], rb[...], cb[...])
    wt_mine[...] = fresh.astype(BF16)

    pl.semaphore_wait(barrier, n)

    def to_pair(slot, src, dst):
        copy = remote(src, dst, pair_send.at[slot], pair_recv.at[slot], me, other)
        copy.start()
        return copy

    def spread_copy(d, out_ref, in_ref, send_sem, recv_sem):
        q = lax.rem(me + d, n)
        return remote(
            out_ref.at[at(q, nb)], in_ref.at[at(me, nb)], send_sem.at[d], recv_sem.at[d], q, r
        )

    def spread_start(*how):
        def go(d, c):
            spread_copy(d, *how).start()
            return c

        lax.fori_loop(1, n, go, 0)

    def spread_wait(out_ref, in_ref, send_sem, recv_sem):
        def go(d, c):
            src = lax.rem(me + n - d, n)
            block = at(src, nb)
            remote(
                out_ref.at[block], in_ref.at[block], send_sem.at[d], recv_sem.at[d], src, r
            ).wait_recv()
            return c

        lax.fori_loop(1, n, go, 0)

    def spread_drain(*how):
        def go(d, c):
            spread_copy(d, *how).wait_send()
            return c

        lax.fori_loop(1, n, go, 0)

    halo = (halo_out, ext.at[pl.ds(nodes, n * nb)], halo_send, halo_recv)
    adj_copy = to_pair(0, adj.at[mine_rows], adj.at[mine_rows])
    cot_copy = to_pair(1, cot.at[:, other_cols], cot_all.at[mine_rows])

    zh = hi // 2
    h = z // zh
    place = lax.rem(z, zh) * lo + l

    def w1_copy(dz):
        q = lax.rem(z + dz, hi) * lo + l
        return remote(
            wt_mine, wt.at[at(place, wrows)], w1_send.at[dz], w_recv.at[place], q, r
        )

    @pl.when(h == r)
    def _():
        for dz in range(1, hi):
            w1_copy(dz).start()
        wt[at(place, wrows), :] = wt_mine[...]

    spread_start(*halo)
    ext[pl.ds(0, nodes), :] = feat[:, mine_cols]
    ext[pl.ds(pl.multiple_of(nodes + me * nb, nb), nb), :] = halo_out[at(me, nb), :]

    adj_copy.wait()
    degree = jnp.sum(adj[...].astype(F32), axis=1, keepdims=True)

    def w_arrival(block):
        here = wt.at[at(block, wrows)]
        return remote(here, here, w1_send.at[0], w_recv.at[block], me, other)

    def w2_copy(i, dl):
        block = i * lo + l
        here = wt.at[at(block, wrows)]
        q = z * lo + lax.rem(l + dl, lo)
        return remote(here, here, w2_send.at[i * lo + dl], w_recv.at[block], q, r)

    for i in range(zh):

        @pl.when(r * zh + i != z)
        def _():
            w_arrival(i * lo + l).wait_recv()

        for dl in range(1, lo):
            w2_copy(i, dl).start()

    spread_wait(*halo)
    agg[:, mine_cols] = (dot(adj[...], ext[...], NN) / degree).astype(BF16)
    agg_copy = to_pair(2, agg.at[:, mine_cols], agg.at[:, mine_cols])

    for i in range(zh):
        for dl in range(1, lo):
            w_arrival(i * lo + lax.rem(l + dl, lo)).wait_recv()
    cot_copy.wait()
    agg_copy.wait()

    preact = dot(agg[...], wt[...], NT)
    sig = jax.nn.sigmoid(preact)
    grad_pre = (cot_all[...].astype(F32) * sig * (1.0 + preact * (1.0 - sig))).astype(BF16)
    mixed = dot(grad_pre, wt[...], NN)
    gm_out[...] = jnp.where(r == 0, mixed[:, half:], mixed[:, :half]).astype(BF16)
    mixed_mine = jnp.where(r == 0, mixed[:, :half], mixed[:, half:])
    gm_copy = to_pair(3, gm_out, gm_in)

    partial = dot(agg[...], grad_pre, TN)
    for p in range(n):
        to = ((p % lo) * hi + p // lo) * wrows
        gw_out[to : to + wrows, :] = partial[p * wrows : (p + 1) * wrows].astype(BF16)
    rows1 = hi * wrows

    def gw1_copy(dl):
        to = lax.rem(l + dl, lo)
        return remote(
            gw_out.at[at(to, rows1)], gw1_in.at[dl], gw1_send.at[dl], gw1_recv.at[dl], z * lo + to, r
        )

    def gw2_copy(dz):
        to = lax.rem(z + dz, hi)
        return remote(
            gw_mid.at[at(to, wrows)], gw2_in.at[dz], gw2_send.at[dz], gw2_recv.at[dz], to * lo + l, r
        )

    for dl in range(1, lo):
        gw1_copy(dl).start()

    gm_copy.wait()
    grad_summed = ((mixed_mine + gm_in[...].astype(F32)) / degree).astype(BF16)
    ret_out[...] = dot(adj[:, nodes:], grad_summed, TN).astype(BF16)
    ret = (ret_out, ret_in, ret_send, ret_recv)
    spread_start(*ret)
    ret_in[at(me, nb), :] = ret_out[at(me, nb), :]
    grad_local = dot(adj[:, :nodes], grad_summed, TN)

    acc = gw_out[at(l, rows1), :].astype(F32)
    for dl in range(1, lo):
        gw1_copy(dl).wait_recv()
        acc = acc + gw1_in[dl].astype(F32)
    gw_mid[...] = acc.astype(BF16)
    for dz in range(1, hi):
        gw2_copy(dz).start()

    spread_wait(*ret)
    total = (grad_local + dot(picks[...], ret_in[...], NN)).astype(BF16)
    fin_out[...] = jnp.where(r == 0, total[TILE:], total[:TILE])
    fin_copy = to_pair(4, fin_out, fin_in)
    out_x[:, mine_cols] = jnp.where(r == 0, total[:TILE], total[TILE:])

    acc = gw_mid[at(z, wrows), :].astype(F32)
    for dz in range(1, hi):
        gw2_copy(dz).wait_recv()
        acc = acc + gw2_in[dz].astype(F32)
    gws_out[...] = jnp.where(r == 0, acc[wsplit:], acc[:wsplit])
    gws_copy = to_pair(5, gws_out, gws_in)
    out_w[:, mine_cols] = jnp.where(r == 0, acc[:wsplit], acc[wsplit:])

    fin_copy.wait()
    out_x[:, other_cols] = fin_in[...]
    gws_copy.wait()
    out_w[:, other_cols] = gws_in[...]

    @pl.when(h == r)
    def _():
        for dz in range(1, hi):
            w1_copy(dz).wait_send()

    for i in range(zh):
        for dl in range(1, lo):
            w2_copy(i, dl).wait_send()
    for dl in range(1, lo):
        gw1_copy(dl).wait_send()
    for dz in range(1, hi):
        gw2_copy(dz).wait_send()
    spread_drain(*halo)
    spread_drain(*ret)


def local(
    features,
    tiles,
    tile_cols,
    tile_count,
    boundary_rows,
    boundary_count,
    cotangent,
    w_init,
    update_map,
    reset_map,
    cand_input,
    cand_hidden,
    update_bias,
    reset_bias,
    cand_bias,
):
    assert features.shape[0] == 1 and tiles.shape[1] == 1
    n = lax.axis_size("dom")
    nodes, width = features.shape[1:]
    half = width // 2
    nb = boundary_rows.shape[-1]
    ncb = (nodes + n * nb) // TILE
    wrows = width // n
    maps = (update_map, reset_map, cand_input, cand_hidden)
    biases = (update_bias.T, reset_bias.T, cand_bias.T)
    state = w_init.T
    if lax.axis_size("snap") > 1:
        state = lax.fori_loop(
            0, lax.axis_index("snap"), lambda i, s: gru_rows(s, *maps, *biases), state
        )

    lo = 4
    hi = n // lo
    zh = hi // 2
    arrays = (features[0], tiles[0, 0], boundary_rows[0, 0], boundary_count[0], cotangent[0], state)
    arrays = arrays + maps + biases
    hbm = pl.BlockSpec(memory_space=pltpu.HBM)
    vmem = pl.BlockSpec(memory_space=pltpu.VMEM)
    smem = pl.BlockSpec(memory_space=pltpu.SMEM)
    dma = pltpu.SemaphoreType.DMA
    out_x, out_w = pl.pallas_call(
        functools.partial(kernel, n, lo),
        out_shape=(
            jax.ShapeDtypeStruct((TILE, width), BF16),
            jax.ShapeDtypeStruct((wrows // 2, width), F32),
        ),
        in_specs=[smem, smem] + [hbm] * len(arrays),
        out_specs=(vmem, vmem),
        scratch_shapes=[pltpu.VMEM(x.shape, x.dtype) for x in arrays]
        + [
            dma((len(arrays),)),
            pltpu.VMEM((nodes, n * nb), BF16),
            pltpu.VMEM((nodes, ncb * TILE), BF16),
            pltpu.VMEM((ncb * TILE, half), BF16),
            pltpu.VMEM((n * nb, half), BF16),
            pltpu.VMEM((nodes, half), BF16),
            pltpu.VMEM((wrows, width), BF16),
            pltpu.VMEM((half, width), BF16),
            pltpu.VMEM((nodes, width), BF16),
            pltpu.VMEM((nodes, half), BF16),
            pltpu.VMEM((nodes, half), BF16),
            pltpu.VMEM((n * nb, half), BF16),
            pltpu.VMEM((n * nb, half), BF16),
            pltpu.VMEM((width, half), BF16),
            pltpu.VMEM((lo, hi * wrows, half), BF16),
            pltpu.VMEM((hi * wrows, half), BF16),
            pltpu.VMEM((hi, wrows, half), BF16),
            pltpu.VMEM((wrows // 2, half), F32),
            pltpu.VMEM((wrows // 2, half), F32),
            pltpu.VMEM((TILE, half), BF16),
            pltpu.VMEM((TILE, half), BF16),
            dma((6,)),
            dma((6,)),
            dma((n,)),
            dma((n,)),
            dma((hi,)),
            dma((zh * lo,)),
            dma((zh * lo,)),
            dma((n,)),
            dma((n,)),
            dma((lo,)),
            dma((lo,)),
            dma((hi,)),
            dma((hi,)),
        ],
        compiler_params=pltpu.CompilerParams(
            collective_id=0, has_side_effects=True, vmem_limit_bytes=60 << 20
        ),
    )(tile_cols[0], tile_count, *arrays)
    return out_x[None], out_w[None]


def solution(mesh):
    in_specs = (
        P("snap", "dom", None),
        P("snap", ("dom", "rep"), None, None, None),
        P("snap", ("dom", "rep"), None),
        P("snap", ("dom", "rep")),
        P("snap", "dom", None, None),
        P("snap", "dom", None),
        P("snap", ("dom", "rep"), None),
        P(None, "dom"),
        P(),
        P(),
        P(),
        P(),
        P(None, "dom"),
        P(None, "dom"),
        P(None, "dom"),
    )
    out_specs = (P("snap", ("dom", "rep"), None), P("snap", ("dom", "rep"), None))
    return jax.shard_map(local, mesh=mesh, in_specs=in_specs, out_specs=out_specs, check_vma=False)
```

```python
import functools

import jax
import jax.numpy as jnp
from jax import lax
from jax.experimental import pallas as pl
from jax.experimental.pallas import tpu as pltpu
from jax.sharding import PartitionSpec as P

TILE = 128
MESH = pl.DeviceIdType.MESH
F32 = jnp.float32
BF16 = jnp.bfloat16


def dot(a, b, dims):
    return lax.dot_general(a, b, (dims, ((), ())), preferred_element_type=F32)


NN = ((1,), (0,))
NT = ((1,), (1,))
TN = ((0,), (0,))


def gru_rows(state, um, rm, ci, ch, ub, rb, cb):
    state_bf = state.astype(BF16)
    update = jax.nn.sigmoid(dot(state_bf, um, NT) + ub)
    reset = jax.nn.sigmoid(dot(state_bf, rm, NT) + rb)
    gated = (reset * state).astype(BF16)
    candidate = jnp.tanh(dot(state_bf, ci, NT) + dot(gated, ch, NT) + cb)
    return (1.0 - update) * state + update * candidate


def kernel(
    n,
    lo,
    cols_hbm,
    count_hbm,
    *refs,
):
    (
        feat_hbm, tiles_hbm, brows_hbm, bcount_hbm, cot_hbm, state_hbm,
        um_hbm, rm_hbm, ci_hbm, ch_hbm, ub_hbm, rb_hbm, cb_hbm,
        out_x, out_w,
        feat, tiles, brows, bcount, cot, state, um, rm, ci, ch, ub, rb, cb,
        in_sem,
        cols_ref, count_ref, scalar_sem, picks, adj, ext, halo_out, cot_all, wt_mine, wt, agg, gm_out, gm_in,
        ret_out, ret_in, gw_out, gw1_in, gw_mid, gw2_in, gws_out, gws_in, fin_out, fin_in,
        pair_send, pair_recv, halo_send, halo_recv, w1_send, w2_send, w_recv,
        ret_send, ret_recv, gw1_send, gw1_recv, gw2_send, gw2_recv,
    ) = refs
    me = lax.axis_index("dom")
    r = lax.axis_index("rep")
    other = 1 - r
    hi = n // lo
    z, l = me // lo, lax.rem(me, lo)
    nodes, width = feat.shape
    half = width // 2
    nb = brows.shape[1]
    wrows = wt_mine.shape[0]
    kmax = tiles.shape[0]
    ncb = adj.shape[1] // TILE
    wsplit = gws_out.shape[0]

    hbm = (feat_hbm, brows_hbm, bcount_hbm, tiles_hbm, cot_hbm, state_hbm,
           um_hbm, rm_hbm, ci_hbm, ch_hbm, ub_hbm, rb_hbm, cb_hbm)
    vmem = (feat, brows, bcount, tiles, cot, state, um, rm, ci, ch, ub, rb, cb)
    loads = [pltpu.make_async_copy(x, y, in_sem.at[i]) for i, (x, y) in enumerate(zip(hbm, vmem))]
    for load in loads:
        load.start()
    scalars = (
        pltpu.make_async_copy(cols_hbm, cols_ref, scalar_sem.at[0]),
        pltpu.make_async_copy(count_hbm, count_ref, scalar_sem.at[1]),
    )
    for load in scalars:
        load.start()

    def cols(which):
        return pl.ds(pl.multiple_of(which * half, half), half)

    def at(i, size):
        return pl.ds(pl.multiple_of(i * size, size), size)

    def remote(src, dst, send_sem, recv_sem, dom, rep):
        return pltpu.make_async_remote_copy(
            src_ref=src,
            dst_ref=dst,
            send_sem=send_sem,
            recv_sem=recv_sem,
            device_id={"dom": dom, "rep": rep},
            device_id_type=MESH,
        )

    mine_rows = at(r, TILE)
    mine_cols, other_cols = cols(r), cols(other)

    barrier = pltpu.get_barrier_semaphore()

    pl.semaphore_signal(barrier, inc=1, device_id={"dom": me, "rep": other}, device_id_type=MESH)

    def greet(i, c):
        q = lax.rem(me + i, n)
        pl.semaphore_signal(barrier, inc=1, device_id={"dom": q, "rep": r}, device_id_type=MESH)
        return c

    lax.fori_loop(1, n, greet, 0)

    for load in loads[:3]:
        load.wait()
    lane = lax.broadcasted_iota(jnp.int32, (nb, n * nb), 1)
    spread_slot = (lax.rem(lane, nb) == lax.broadcasted_iota(jnp.int32, (nb, n * nb), 0)).astype(F32)
    lane_q = lax.broadcasted_iota(jnp.int32, (n, n * nb), 1)
    in_q = lax.div(lane_q, nb) == lax.broadcasted_iota(jnp.int32, (n, n * nb), 0)
    by_slot = dot(brows[...].astype(F32).astype(BF16), spread_slot.astype(BF16), NN)
    row_of = jnp.sum(jnp.where(in_q, by_slot, 0.0), axis=0, keepdims=True)
    counts = jnp.broadcast_to(bcount[...].astype(F32), (n, n)).astype(BF16)
    limit = dot(counts, in_q.astype(F32).astype(BF16), NN)[0:1]
    slot = lax.rem(lane_q[0:1], nb).astype(F32)
    rowsel = jnp.where(slot < limit, row_of, -1.0).astype(jnp.int32)
    picks[...] = (lax.broadcasted_iota(jnp.int32, (nodes, n * nb), 0) == rowsel).astype(F32).astype(BF16)
    halo_out[...] = dot(picks[...], feat[:, mine_cols], TN).astype(BF16)

    for load in loads[3:5] + list(scalars):
        load.wait()
    for c in range(ncb):
        index = jnp.int32(0)
        live = jnp.float32(0.0)
        for k in range(kmax):
            hit = (cols_ref[0, k] == c) & (k < count_ref[0, 0])
            index = jnp.where(hit, k, index)
            live = jnp.where(hit, 1.0, live)
        adj[mine_rows, c * TILE : (c + 1) * TILE] = (tiles[index].astype(F32) * live).astype(BF16)
    cot_all[mine_rows, :] = cot[:, mine_cols]

    for load in loads[5:]:
        load.wait()
    fresh = gru_rows(state[...], um[...], rm[...], ci[...], ch[...], ub[...], rb[...], cb[...])
    wt_mine[...] = fresh.astype(BF16)

    pl.semaphore_wait(barrier, n)

    def to_pair(slot, src, dst):
        copy = remote(src, dst, pair_send.at[slot], pair_recv.at[slot], me, other)
        copy.start()
        return copy

    def spread_copy(d, out_ref, in_ref, send_sem, recv_sem):
        q = lax.rem(me + d, n)
        return remote(
            out_ref.at[at(q, nb)], in_ref.at[at(me, nb)], send_sem.at[d], recv_sem.at[d], q, r
        )

    def spread_start(*how):
        def go(d, c):
            spread_copy(d, *how).start()
            return c

        lax.fori_loop(1, n, go, 0)

    def spread_wait(out_ref, in_ref, send_sem, recv_sem):
        def go(d, c):
            src = lax.rem(me + n - d, n)
            block = at(src, nb)
            remote(
                out_ref.at[block], in_ref.at[block], send_sem.at[d], recv_sem.at[d], src, r
            ).wait_recv()
            return c

        lax.fori_loop(1, n, go, 0)

    def spread_drain(*how):
        def go(d, c):
            spread_copy(d, *how).wait_send()
            return c

        lax.fori_loop(1, n, go, 0)

    halo = (halo_out, ext.at[pl.ds(nodes, n * nb)], halo_send, halo_recv)
    adj_copy = to_pair(0, adj.at[mine_rows], adj.at[mine_rows])
    cot_copy = to_pair(1, cot.at[:, other_cols], cot_all.at[mine_rows])

    zh = hi // 2
    h = z // zh
    place = lax.rem(z, zh) * lo + l

    def w1_copy(dz):
        q = lax.rem(z + dz, hi) * lo + l
        return remote(
            wt_mine, wt.at[at(place, wrows)], w1_send.at[dz], w_recv.at[place], q, r
        )

    @pl.when(h == r)
    def _():
        for dz in range(1, hi):
            w1_copy(dz).start()
        wt[at(place, wrows), :] = wt_mine[...]

    spread_start(*halo)
    ext[pl.ds(0, nodes), :] = feat[:, mine_cols]
    ext[pl.ds(pl.multiple_of(nodes + me * nb, nb), nb), :] = halo_out[at(me, nb), :]

    adj_copy.wait()
    degree = jnp.sum(adj[...].astype(F32), axis=1, keepdims=True)

    def w_arrival(block):
        here = wt.at[at(block, wrows)]
        return remote(here, here, w1_send.at[0], w_recv.at[block], me, other)

    def w2_copy(i, dl):
        block = i * lo + l
        here = wt.at[at(block, wrows)]
        q = z * lo + lax.rem(l + dl, lo)
        return remote(here, here, w2_send.at[i * lo + dl], w_recv.at[block], q, r)

    for i in range(zh):

        @pl.when(r * zh + i != z)
        def _():
            w_arrival(i * lo + l).wait_recv()

        for dl in range(1, lo):
            w2_copy(i, dl).start()

    spread_wait(*halo)
    agg[:, mine_cols] = (dot(adj[...], ext[...], NN) / degree).astype(BF16)
    agg_copy = to_pair(2, agg.at[:, mine_cols], agg.at[:, mine_cols])

    for i in range(zh):
        for dl in range(1, lo):
            w_arrival(i * lo + lax.rem(l + dl, lo)).wait_recv()
    cot_copy.wait()
    agg_copy.wait()

    preact = dot(agg[...], wt[...], NT)
    sig = jax.nn.sigmoid(preact)
    grad_pre = (cot_all[...].astype(F32) * sig * (1.0 + preact * (1.0 - sig))).astype(BF16)
    mixed = dot(grad_pre, wt[...], NN)
    gm_out[...] = jnp.where(r == 0, mixed[:, half:], mixed[:, :half]).astype(BF16)
    mixed_mine = jnp.where(r == 0, mixed[:, :half], mixed[:, half:])
    gm_copy = to_pair(3, gm_out, gm_in)

    partial = dot(agg[...], grad_pre, TN)
    for p in range(n):
        to = ((p % lo) * hi + p // lo) * wrows
        gw_out[to : to + wrows, :] = partial[p * wrows : (p + 1) * wrows].astype(BF16)
    rows1 = hi * wrows

    def gw1_copy(dl):
        to = lax.rem(l + dl, lo)
        return remote(
            gw_out.at[at(to, rows1)], gw1_in.at[dl], gw1_send.at[dl], gw1_recv.at[dl], z * lo + to, r
        )

    def gw2_copy(dz):
        to = lax.rem(z + dz, hi)
        return remote(
            gw_mid.at[at(to, wrows)], gw2_in.at[dz], gw2_send.at[dz], gw2_recv.at[dz], to * lo + l, r
        )

    for dl in range(1, lo):
        gw1_copy(dl).start()

    gm_copy.wait()
    grad_summed = ((mixed_mine + gm_in[...].astype(F32)) / degree).astype(BF16)
    ret = (ret_out, ret_in, ret_send, ret_recv)
    per_tile = TILE // nb
    tiles_all = n // per_tile

    def send_tile(t):
        tile_no = lax.rem(me // per_tile + 1 + t, tiles_all)
        piece = dot(adj[:, pl.ds(pl.multiple_of(nodes + tile_no * TILE, TILE), TILE)], grad_summed, TN)
        ret_out[at(tile_no, TILE), :] = piece.astype(BF16)
        for i in range(per_tile):
            q = tile_no * per_tile + lax.rem(me + i, per_tile)

            @pl.when(q != me)
            def _():
                spread_copy(lax.rem(q - me + n, n), *ret).start()

    for t in range(tiles_all):
        send_tile(t)
    ret_in[at(me, nb), :] = ret_out[at(me, nb), :]
    grad_local = dot(adj[:, :nodes], grad_summed, TN)

    acc = gw_out[at(l, rows1), :].astype(F32)
    for dl in range(1, lo):
        gw1_copy(dl).wait_recv()
        acc = acc + gw1_in[dl].astype(F32)
    gw_mid[...] = acc.astype(BF16)
    for dz in range(1, hi):
        gw2_copy(dz).start()

    spread_wait(*ret)
    total = (grad_local + dot(picks[...], ret_in[...], NN)).astype(BF16)
    fin_out[...] = jnp.where(r == 0, total[TILE:], total[:TILE])
    fin_copy = to_pair(4, fin_out, fin_in)
    out_x[:, mine_cols] = jnp.where(r == 0, total[:TILE], total[TILE:])

    acc = gw_mid[at(z, wrows), :].astype(F32)
    for dz in range(1, hi):
        gw2_copy(dz).wait_recv()
        acc = acc + gw2_in[dz].astype(F32)
    gws_out[...] = jnp.where(r == 0, acc[wsplit:], acc[:wsplit])
    gws_copy = to_pair(5, gws_out, gws_in)
    out_w[:, mine_cols] = jnp.where(r == 0, acc[:wsplit], acc[wsplit:])

    fin_copy.wait()
    out_x[:, other_cols] = fin_in[...]
    gws_copy.wait()
    out_w[:, other_cols] = gws_in[...]

    @pl.when(h == r)
    def _():
        for dz in range(1, hi):
            w1_copy(dz).wait_send()

    for i in range(zh):
        for dl in range(1, lo):
            w2_copy(i, dl).wait_send()
    for dl in range(1, lo):
        gw1_copy(dl).wait_send()
    for dz in range(1, hi):
        gw2_copy(dz).wait_send()
    spread_drain(*halo)
    spread_drain(*ret)


def store(x_ref, w_ref, x_out, w_out, sem):
    copies = (
        pltpu.make_async_copy(x_ref, x_out, sem.at[0]),
        pltpu.make_async_copy(w_ref, w_out, sem.at[1]),
    )
    for copy in copies:
        copy.start()
    for copy in copies:
        copy.wait()


def local(
    features,
    tiles,
    tile_cols,
    tile_count,
    boundary_rows,
    boundary_count,
    cotangent,
    w_init,
    update_map,
    reset_map,
    cand_input,
    cand_hidden,
    update_bias,
    reset_bias,
    cand_bias,
):
    assert features.shape[0] == 1 and tiles.shape[1] == 1
    n = lax.axis_size("dom")
    nodes, width = features.shape[1:]
    half = width // 2
    nb = boundary_rows.shape[-1]
    ncb = (nodes + n * nb) // TILE
    wrows = width // n
    maps = (update_map, reset_map, cand_input, cand_hidden)
    biases = (update_bias.T, reset_bias.T, cand_bias.T)
    state = w_init.T
    if lax.axis_size("snap") > 1:
        state = lax.fori_loop(
            0, lax.axis_index("snap"), lambda i, s: gru_rows(s, *maps, *biases), state
        )

    lo = 4
    hi = n // lo
    zh = hi // 2
    arrays = (features[0], tiles[0, 0], boundary_rows[0, 0], boundary_count[0], cotangent[0], state)
    arrays = arrays + maps + biases
    hbm = pl.BlockSpec(memory_space=pltpu.HBM)
    vmem = pl.BlockSpec(memory_space=pltpu.VMEM)
    dma = pltpu.SemaphoreType.DMA
    out_x, out_w = pl.pallas_call(
        functools.partial(kernel, n, lo),
        out_shape=(
            jax.ShapeDtypeStruct((TILE, width), BF16),
            jax.ShapeDtypeStruct((wrows // 2, width), F32),
        ),
        in_specs=[hbm] * (len(arrays) + 2),
        out_specs=(vmem, vmem),
        scratch_shapes=[pltpu.VMEM(x.shape, x.dtype) for x in arrays]
        + [
            dma((len(arrays),)),
            pltpu.SMEM((1, tile_cols.shape[2]), jnp.int32),
            pltpu.SMEM((1, 1), jnp.int32),
            dma((2,)),
            pltpu.VMEM((nodes, n * nb), BF16),
            pltpu.VMEM((nodes, ncb * TILE), BF16),
            pltpu.VMEM((ncb * TILE, half), BF16),
            pltpu.VMEM((n * nb, half), BF16),
            pltpu.VMEM((nodes, half), BF16),
            pltpu.VMEM((wrows, width), BF16),
            pltpu.VMEM((half, width), BF16),
            pltpu.VMEM((nodes, width), BF16),
            pltpu.VMEM((nodes, half), BF16),
            pltpu.VMEM((nodes, half), BF16),
            pltpu.VMEM((n * nb, half), BF16),
            pltpu.VMEM((n * nb, half), BF16),
            pltpu.VMEM((width, half), BF16),
            pltpu.VMEM((lo, hi * wrows, half), BF16),
            pltpu.VMEM((hi * wrows, half), BF16),
            pltpu.VMEM((hi, wrows, half), BF16),
            pltpu.VMEM((wrows // 2, half), F32),
            pltpu.VMEM((wrows // 2, half), F32),
            pltpu.VMEM((TILE, half), BF16),
            pltpu.VMEM((TILE, half), BF16),
            dma((6,)),
            dma((6,)),
            dma((n,)),
            dma((n,)),
            dma((hi,)),
            dma((zh * lo,)),
            dma((zh * lo,)),
            dma((n,)),
            dma((n,)),
            dma((lo,)),
            dma((lo,)),
            dma((hi,)),
            dma((hi,)),
        ],
        compiler_params=pltpu.CompilerParams(
            collective_id=0, has_side_effects=True, vmem_limit_bytes=60 << 20
        ),
    )(tile_cols[0], tile_count, *arrays)
    out_x, out_w = pl.pallas_call(
        store,
        out_shape=(
            jax.ShapeDtypeStruct(out_x.shape, BF16),
            jax.ShapeDtypeStruct(out_w.shape, F32),
        ),
        in_specs=[vmem, vmem],
        out_specs=(hbm, hbm),
        scratch_shapes=[dma((2,))],
    )(out_x, out_w)
    return out_x[None], out_w[None]


def solution(mesh):
    in_specs = (
        P("snap", "dom", None),
        P("snap", ("dom", "rep"), None, None, None),
        P("snap", ("dom", "rep"), None),
        P("snap", ("dom", "rep")),
        P("snap", "dom", None, None),
        P("snap", "dom", None),
        P("snap", ("dom", "rep"), None),
        P(None, "dom"),
        P(),
        P(),
        P(),
        P(),
        P(None, "dom"),
        P(None, "dom"),
        P(None, "dom"),
    )
    out_specs = (P("snap", ("dom", "rep"), None), P("snap", ("dom", "rep"), None))
    return jax.shard_map(local, mesh=mesh, in_specs=in_specs, out_specs=out_specs, check_vma=False)
```
